768 devices in a mesh: shard: 32 (over x, y), rep: 24 (over z, core).
Axes of the slice: x: 4, y: 8, z: 12, core: 2. Of those that a mesh axis runs over, the one named last changes fastest.
Arguments:
- acts: bfloat16 [24, 384, 96, 512], P('rep', 'shard'), may hold values from -70 to 70, as said below
- cotangents: bfloat16 [24, 384, 96, 512], P('rep', 'shard'), may hold values from -6 to 6
- block_shapes: int32 [384, 2], P('shard'), may hold values from 128 to 512, as said below
- owners: int32 [768], P('shard'), may hold values from 0 to 23, as said below
Outputs:
- updates: float32 [32, 24, 256, 512], P(None, 'rep', 'shard')
The draws below stay inside these ranges and needn't reach their ends.
Inputs may be any that keep to these rules, and one draw needn't show every extreme that they name: `acts`: each layer input is within the range; feature columns have different scales. `block_shapes`: live rows and columns of a block; some blocks are full in every draw. Within each group of 24 consecutive factors (factor k of the group, k from 0), owners equals (k + c) mod 24 for one number c of that group.
All inputs are finite; a program needn't handle non-finite values.
Results may differ from the reference program's by a relative error of at most 0.015.
Values may be sent and summed in bfloat16 or wider, within the bound.
A program may use at most 32 MiB of HBM per device.

```python
import math
import jax
import jax.numpy as jnp
from jax import lax

B = 512
TOK = 96
ITERS = 2
KB = 12
NBLK = 384
NFAC = 768
HALF = 256
N_SHARD = 32
N_REP = 24


def draw_acts(key, part):
    key = jax.random.fold_in(key, 11)
    key_values, key_columns = jax.random.split(key, 2)
    column_scale = jnp.exp(jax.random.uniform(key_columns, (1, 1, 1, B), jnp.float32, 0.0, math.log(10.0)))
    values = jax.random.truncated_normal(key_values, -4.0, 4.0, (N_REP, NBLK, TOK, B), jnp.float32)
    return (values * column_scale).astype(jnp.bfloat16)


def draw_block_shapes(key, part):
    key = jax.random.fold_in(key, 12)
    key_ragged, key_pick = jax.random.split(key)
    ragged = jax.random.randint(key_ragged, (NBLK, 2), B // 4, B)
    pick = jax.random.randint(key_pick, (NBLK, 2), 0, 4)
    values = jnp.where(pick == 0, ragged, B)
    return values.at[0].set(B).astype(jnp.int32)


def draw_owners(key, part):
    key = jax.random.fold_in(key, 13)
    rotations = jax.random.randint(key, (N_SHARD,), 0, N_REP)
    local_index = jnp.arange(NFAC, dtype=jnp.int32) % N_REP
    return ((local_index + jnp.repeat(rotations, N_REP)) % N_REP).astype(jnp.int32)


def steps_of(rng, dims, shards, least, high):
    def one(dim, parts):
        draws = jax.random.uniform(jax.random.fold_in(jax.random.fold_in(rng, 6), dim), (parts,), jnp.float32, least / len(shards), high / len(shards))
        return jnp.repeat(jnp.exp(draws), dims[dim] // parts).reshape((-1,) + (1,) * (len(dims) - dim - 1))

    level = one(*shards[0])
    for cut in shards[1:]:
        level = level * one(*cut)
    return level


def noise(rng, extent, deviation, reach, cuts=(), held_as=jnp.bfloat16):
    values = jax.random.normal(rng, extent, jnp.float32) * deviation
    if len(cuts) > 0:
        values = steps_of(rng, extent, cuts, -0.22, 0.18) * values
    return jnp.clip(values, min=-reach, max=reach).astype(held_as)


def setup_inputs(seed: int = 0) -> dict:
    splits = jax.random.split(jax.random.key(seed), 5)
    acts = draw_acts(jax.random.fold_in(splits[4], 71), 0)
    cotangents = noise(splits[1], (N_REP, NBLK, TOK, B), 1.0, 6.0, ((0, 24), (1, 32)))
    block_shapes = draw_block_shapes(jax.random.fold_in(splits[4], 71), 0)
    owners = draw_owners(jax.random.fold_in(splits[4], 71), 0)
    return {"acts": acts, "cotangents": cotangents, "block_shapes": block_shapes, "owners": owners}


damping_ratio = 0.01

def inverse_root(stat):
    identity = jnp.eye(B, dtype=jnp.float32)
    damped = stat + damping_ratio * (jnp.trace(stat) / B + 1e-06) * identity
    scale_norm = jnp.sqrt(jnp.sum(damped * damped))
    coupled = damped / scale_norm
    estimate = identity * scale_norm ** (-0.25)
    for iteration in range(ITERS):
        factor = (5.0 * identity - coupled) / 4.0
        estimate = jnp.dot(estimate, factor, precision=lax.Precision.HIGHEST)
        square = jnp.dot(factor, factor, precision=lax.Precision.HIGHEST)
        fourth = jnp.dot(square, square, precision=lax.Precision.HIGHEST)
        coupled = jnp.dot(fourth, coupled, precision=lax.Precision.HIGHEST)
    return estimate.astype(jnp.bfloat16)

def one_block(acts_block, cots_block, limits):
    column = jnp.arange(B, dtype=jnp.int32)
    half_tok = TOK // 2
    inputs = jnp.where(column < limits[0], acts_block, 0)
    outputs = jnp.where(column < limits[1], cots_block, 0)
    first = jnp.dot(inputs[:, :half_tok].reshape(-1, B).T, outputs[:, :half_tok].reshape(-1, B), preferred_element_type=jnp.float32).astype(jnp.bfloat16)
    second = jnp.dot(inputs[:, half_tok:].reshape(-1, B).T, outputs[:, half_tok:].reshape(-1, B), preferred_element_type=jnp.float32).astype(jnp.bfloat16)
    gradient = first.astype(jnp.float32) + second.astype(jnp.float32)
    grad_bf = gradient.astype(jnp.bfloat16)
    left_root = inverse_root(jnp.dot(grad_bf, grad_bf.T, preferred_element_type=jnp.float32))
    right_root = inverse_root(jnp.dot(grad_bf.T, grad_bf, preferred_element_type=jnp.float32))
    product = jnp.dot(left_root, grad_bf, preferred_element_type=jnp.float32).astype(jnp.bfloat16)
    return math.sqrt(B) * jnp.dot(product, right_root, preferred_element_type=jnp.float32)

def one_group(group_args):
    acts_group, cots_group, shapes_group, owners_group = group_args
    blocks_out = jax.vmap(one_block, in_axes=(1, 1, 0))(acts_group, cots_group, shapes_group)
    halves = blocks_out.reshape(KB * 2, HALF, B)
    return jnp.zeros((N_REP, HALF, B), jnp.float32).at[owners_group].set(halves)

def reference(acts, cotangents, block_shapes, owners):
    acts_grouped = acts.reshape(N_REP, N_SHARD, KB, TOK, B).transpose(1, 0, 2, 3, 4)
    cots_grouped = cotangents.reshape(N_REP, N_SHARD, KB, TOK, B).transpose(1, 0, 2, 3, 4)
    shapes_grouped = block_shapes.reshape(N_SHARD, KB, 2)
    owners_grouped = owners.reshape(N_SHARD, N_REP)
    return lax.map(one_group, (acts_grouped, cots_grouped, shapes_grouped, owners_grouped))
```

```python
import functools
import math

import jax
import jax.numpy as jnp
from jax import lax
from jax.experimental import pallas as pl
from jax.experimental.pallas import tpu as pltpu
from jax.sharding import PartitionSpec as P

MESH = pl.DeviceIdType.MESH
DAMPING = 0.01
CHUNKS = 4
STRIPS = 4

ROWS_BY_ROWS = (((1,), (1,)), ((), ()))
COLUMNS_BY_COLUMNS = (((0,), (0,)), ((), ()))


def dot(a, b, dims=(((1,), (0,)), ((), ()))):
    return lax.dot_general(a, b, dims, preferred_element_type=jnp.float32)


def kernel(
    n_z, n_x, n_y,
    owners_ref, shapes_ref, acts_ref, cots_ref, out_ref,
    staged, paired, part_long, part_short, in_long, in_short, grad,
    stat, coupled, coupled_bf, work, work_bf, left, right,
    weighted, weighted_out, rows_own, rows_shift, rows_out, landing,
    pair_send, pair_recv, long_send, long_recv, short_send, short_recv,
    grad_send, grad_recv, root_send, root_recv, shift_send, shift_recv, rows_send, rows_recv,
):
    width = acts_ref.shape[3]
    tokens = acts_ref.shape[2]
    half = width // 2
    n_shard = n_x * n_y
    n_long = n_z // 2
    n_short = n_z - 1 - n_long
    shard = lax.axis_index("shard")
    rep = lax.axis_index("rep")
    z = rep // 2
    core = rep % 2
    x = shard // n_y
    y = shard % n_y
    sign = 1 - 2 * core
    partner = (shard, z * 2 + 1 - core)
    long_to = (shard, lax.rem(z + sign + n_z, n_z) * 2 + core)
    short_to = (shard, lax.rem(z - sign + n_z, n_z) * 2 + core)
    shift_to = (shard, lax.rem(z + 1, n_z) * 2 + core)
    shift_from = (shard, lax.rem(z + n_z - 1, n_z) * 2 + core)

    def peer(across, along):
        return lax.rem(x + across, n_x) * n_y + lax.rem(y + along, n_y)

    def source(across, along):
        return lax.rem(x + n_x - across, n_x) * n_y + lax.rem(y + n_y - along, n_y)

    barrier = pltpu.get_barrier_semaphore()
    for neighbour in (partner, long_to, short_to):
        pl.semaphore_signal(barrier, inc=1, device_id=neighbour, device_id_type=MESH)

    @pl.loop(1, n_shard)
    def _(step):
        to = (peer(step // n_y, lax.rem(step, n_y)), rep)
        pl.semaphore_signal(barrier, inc=1, device_id=to, device_id_type=MESH)

    rotation = owners_ref[0]
    turn = lax.div(rotation, 2)
    odd = (rotation - 2 * turn).astype(jnp.float32)
    even = 1.0 - odd

    def block_of(chip):
        return lax.rem(chip + 2 * n_z - turn, n_z)

    def hops(item):
        pair, second = lax.div(item, 2), lax.rem(item, 2)
        return (1 - second) * (n_long - pair) - second * (n_short - pair)

    own_columns = pl.ds(pl.multiple_of(core * half, half), half)
    other_columns = pl.ds(pl.multiple_of((1 - core) * half, half), half)

    @pl.loop(0, n_z)
    def _(item):
        block = block_of(lax.rem(z - sign * hops(item) + n_z, n_z))
        staged[item, :, :width] = cots_ref[0, block]
        staged[item, :, width:] = acts_ref[0, block, :, other_columns]

    def pair_copy(item):
        return pltpu.make_async_remote_copy(
            src_ref=staged.at[item],
            dst_ref=paired.at[item, pl.ds(tokens, tokens), :],
            send_sem=pair_send.at[item],
            recv_sem=pair_recv.at[item],
            device_id=partner,
            device_id_type=MESH,
        )

    pl.semaphore_wait(barrier, 3 + n_shard - 1)

    @pl.loop(0, n_z)
    def _(item):
        pair_copy(item).start()

    @pl.loop(0, n_z)
    def _(item):
        block = block_of(lax.rem(z + sign * hops(item) + n_z, n_z))
        paired[item, :tokens, :width] = cots_ref[0, block]
        paired[item, :tokens, width:] = acts_ref[0, block, :, own_columns]

    def partial(item, into):
        pair_copy(item).wait_recv()
        into[...] = dot(paired[item, :, width:], paired[item, :, :width], COLUMNS_BY_COLUMNS)

    rows = half // CHUNKS

    def ring_copy(buffer, send, recv, to, step, chunk):
        return pltpu.make_async_remote_copy(
            src_ref=buffer.at[step, pl.ds(chunk * rows, rows), :],
            dst_ref=buffer.at[step + 1, pl.ds(chunk * rows, rows), :],
            send_sem=send.at[step, chunk],
            recv_sem=recv.at[step, chunk],
            device_id=to,
            device_id_type=MESH,
        )

    long_copy = functools.partial(ring_copy, in_long, long_send, long_recv, long_to)
    short_copy = functools.partial(ring_copy, in_short, short_send, short_recv, short_to)

    partial(0, part_long)
    for chunk in range(CHUNKS):
        span = pl.ds(chunk * rows, rows)
        in_long[0, span, :] = part_long[span, :].astype(jnp.bfloat16)
        long_copy(0, chunk).start()
    partial(1, part_short)
    for chunk in range(CHUNKS):
        span = pl.ds(chunk * rows, rows)
        in_short[0, span, :] = part_short[span, :].astype(jnp.bfloat16)
        short_copy(0, chunk).start()

    def forward(buffer, part, copy, step, chunk):
        span = pl.ds(chunk * rows, rows)
        copy(step - 1, chunk).wait_recv()
        total = buffer[step, span, :].astype(jnp.float32) + part[span, :]
        buffer[step, span, :] = total.astype(jnp.bfloat16)
        copy(step, chunk).start()

    @pl.loop(1, n_short)
    def _(step):
        partial(2 * step, part_long)
        partial(2 * step + 1, part_short)
        for chunk in range(CHUNKS):
            forward(in_long, part_long, long_copy, step, chunk)
            forward(in_short, part_short, short_copy, step, chunk)

    partial(2 * n_long - 2, part_long)
    partial(2 * n_long - 1, part_short)
    for chunk in range(CHUNKS):
        forward(in_long, part_long, long_copy, n_long - 1, chunk)

    own_block = block_of(z)
    live_rows = shapes_ref[own_block, 0]
    live_columns = shapes_ref[own_block, 1]

    def grad_copy(chunk):
        span = pl.ds(pl.multiple_of(core * half + chunk * rows, rows), rows)
        return pltpu.make_async_remote_copy(
            src_ref=grad.at[span, :],
            dst_ref=grad.at[span, :],
            send_sem=grad_send.at[chunk],
            recv_sem=grad_recv.at[chunk],
            device_id=partner,
            device_id_type=MESH,
        )

    for chunk in range(CHUNKS):
        span = pl.ds(chunk * rows, rows)
        short_copy(n_short - 1, chunk).wait_recv()
        total = part_short[span, :] + in_short[n_short, span, :].astype(jnp.float32)
        long_copy(n_long - 1, chunk).wait_recv()
        total = total + in_long[n_long, span, :].astype(jnp.float32)
        first = core * half + chunk * rows
        below = live_rows - first - lax.broadcasted_iota(jnp.int32, (rows, width), 0)
        before = live_columns - lax.broadcasted_iota(jnp.int32, (rows, width), 1)
        live = jnp.minimum(jnp.maximum(jnp.minimum(below, before), 0), 1)
        total = total * live.astype(jnp.float32)
        grad[pl.ds(pl.multiple_of(first, rows), rows), :] = total.astype(jnp.bfloat16)
        grad_copy(chunk).start()
    for chunk in range(CHUNKS):
        grad_copy(chunk).wait_recv()

    deep = width // STRIPS
    strips = [slice(i * deep, (i + 1) * deep) for i in range(STRIPS)]

    @pl.when(core == 0)
    def _():
        for strip in strips:
            stat[strip, :] = dot(grad[strip, :], grad[...], ROWS_BY_ROWS)

    @pl.when(core == 1)
    def _():
        for strip in strips:
            stat[strip, :] = dot(grad[:, strip], grad[...], COLUMNS_BY_COLUMNS)

    def diagonal(strip):
        return (
            lax.broadcasted_iota(jnp.int32, (deep, width), 0) + strip.start
            == lax.broadcasted_iota(jnp.int32, (deep, width), 1)
        )

    squares = jnp.zeros((1, 1), jnp.float32)
    trace = jnp.zeros((1, 1), jnp.float32)
    for strip in strips:
        values = stat[strip, :]
        squares += jnp.sum(values * values, keepdims=True)
        trace += jnp.sum(jnp.where(diagonal(strip), values, 0.0), keepdims=True)
    damping = DAMPING * (trace / width + 1e-06)
    norm_squared = squares + damping * (2.0 * trace + width * damping)
    inverse = lax.rsqrt(norm_squared)
    scale = lax.rsqrt(jnp.sqrt(jnp.sqrt(norm_squared)))

    for strip in strips:
        values = (stat[strip, :] + jnp.where(diagonal(strip), damping, 0.0)) * inverse
        coupled[strip, :] = values
        coupled_bf[strip, :] = values.astype(jnp.bfloat16)
    for strip in strips:
        square = dot(coupled_bf[strip, :], coupled_bf[...])
        values = 0.0625 * square - 0.625 * coupled[strip, :]
        stat[strip, :] = values
        work_bf[0, strip, :] = values.astype(jnp.bfloat16)
    for strip in strips:
        square = dot(work_bf[0, strip, :], work_bf[0])
        work_bf[1, strip, :] = (square + 3.125 * stat[strip, :]).astype(jnp.bfloat16)
    for strip in strips:
        values = dot(work_bf[1, strip, :], coupled_bf[...]) + 2.44140625 * coupled[strip, :]
        work[strip, :] = values
        work_bf[0, strip, :] = values.astype(jnp.bfloat16)

    def root(strip):
        values = 0.0625 * dot(coupled_bf[strip, :], work_bf[0])
        values = values - 0.3125 * (coupled[strip, :] + work[strip, :])
        values = values + jnp.where(diagonal(strip), 1.5625, 0.0)
        return (values * scale).astype(jnp.bfloat16)

    def right_copy(index):
        span = pl.ds(index * deep, deep)
        return pltpu.make_async_remote_copy(
            src_ref=right.at[span, :],
            dst_ref=right.at[span, :],
            send_sem=root_send.at[index],
            recv_sem=root_recv.at[index],
            device_id=partner,
            device_id_type=MESH,
        )

    weighted_copy = pltpu.make_async_remote_copy(
        src_ref=weighted_out,
        dst_ref=weighted,
        send_sem=root_send.at[STRIPS],
        recv_sem=root_recv.at[STRIPS],
        device_id=partner,
        device_id_type=MESH,
    )

    @pl.when(core == 1)
    def _():
        for index, strip in enumerate(strips):
            right[strip, :] = root(strip)
            right_copy(index).start()
        weighted_copy.wait_recv()

    @pl.when(core == 0)
    def _():
        for strip in strips:
            left[strip, :] = root(strip)
        upper = left[:half, :].astype(jnp.float32)
        lower = left[half:, :].astype(jnp.float32)
        given = (upper * odd + lower * even).astype(jnp.bfloat16)
        weighted_out[...] = dot(given, grad[...]).astype(jnp.bfloat16)
        weighted_copy.start()
        kept = (upper * even + lower * odd).astype(jnp.bfloat16)
        weighted[...] = dot(kept, grad[...]).astype(jnp.bfloat16)
        for index in range(STRIPS):
            right_copy(index).wait_recv()

    piece = half // n_shard
    spread = half // n_x

    def update_rows(across):
        start = pl.multiple_of(lax.rem(x + across, n_x) * spread, spread)
        values = dot(weighted[pl.ds(start, spread), :], right[...]) * math.sqrt(width)
        values = values.reshape(n_y, piece, width)
        values = jnp.concatenate([values[:, :, :half], values[:, :, half:]], axis=1)
        return values.astype(jnp.bfloat16)

    def places(across):
        start = pl.multiple_of(lax.rem(x + across, n_x) * n_y, n_y)
        return pl.ds(start, n_y)

    def shift_copy(across):
        return pltpu.make_async_remote_copy(
            src_ref=rows_own.at[places(across)],
            dst_ref=rows_shift.at[places(across)],
            send_sem=shift_send.at[across],
            recv_sem=shift_recv.at[across],
            device_id=shift_to,
            device_id_type=MESH,
        )

    def rows_copy(across, along):
        return pltpu.make_async_remote_copy(
            src_ref=rows_out.at[peer(across, along)],
            dst_ref=landing.at[shard],
            send_sem=rows_send.at[across, along],
            recv_sem=rows_recv.at[across, along],
            device_id=(peer(across, along), rep),
            device_id_type=MESH,
        )

    def spread_rows(across):
        if across == 0:
            landing[shard] = rows_out[shard]

        @pl.loop(1 if across == 0 else 0, n_y)
        def _(along):
            rows_copy(across, along).start()

    @pl.when(core == 1)
    def _():
        for across in range(n_x):
            rows_out[places(across)] = update_rows(across)
            spread_rows(across)

    @pl.when(core == 0)
    def _():
        for across in range(n_x):
            rows_own[places(across)] = update_rows(across)
            shift_copy(across).start()
        for across in range(n_x):
            shift_copy(across).wait_recv()
            moved = rows_shift[places(across)].astype(jnp.float32)
            values = moved * odd + rows_own[places(across)].astype(jnp.float32) * even
            rows_out[places(across)] = values.astype(jnp.bfloat16)
            spread_rows(across)

    def unfold(place):
        values = landing[place].astype(jnp.float32)
        out_ref[place, 0, :, :half] = values[:piece]
        out_ref[place, 0, :, half:] = values[piece:]

    unfold(shard)

    @pl.loop(1, n_shard)
    def _(step):
        across, along = step // n_y, lax.rem(step, n_y)
        rows_copy(across, along).wait_recv()
        unfold(source(across, along))

    @pl.loop(0, n_z)
    def _(item):
        pair_copy(item).wait_send()

    @pl.loop(0, n_long)
    def _(step):
        for chunk in range(CHUNKS):
            long_copy(step, chunk).wait_send()

    @pl.loop(0, n_short)
    def _(step):
        for chunk in range(CHUNKS):
            short_copy(step, chunk).wait_send()

    for chunk in range(CHUNKS):
        grad_copy(chunk).wait_send()

    @pl.when(core == 1)
    def _():
        for index in range(STRIPS):
            right_copy(index).wait_send()

    @pl.when(core == 0)
    def _():
        weighted_copy.wait_send()
        for across in range(n_x):
            shift_copy(across).wait_send()

    @pl.loop(1, n_shard)
    def _(step):
        rows_copy(step // n_y, lax.rem(step, n_y)).wait_send()


def local(n_shard, n_rep, acts, cotangents, block_shapes, owners):
    n_z = n_rep // 2
    n_x = 4 if n_shard == 32 else 1
    n_y = n_shard // n_x
    tokens, width = acts.shape[2:]
    half = width // 2
    n_long = n_z // 2
    n_short = n_z - 1 - n_long
    piece = half // n_shard
    bf16, f32 = jnp.bfloat16, jnp.float32
    dma = pltpu.SemaphoreType.DMA
    pieces = pltpu.VMEM((n_shard, 2 * piece, half), bf16)
    return pl.pallas_call(
        functools.partial(kernel, n_z, n_x, n_y),
        out_shape=jax.ShapeDtypeStruct((n_shard, 1, piece, width), f32),
        in_specs=[pl.BlockSpec(memory_space=pltpu.SMEM)] * 2 + [pl.BlockSpec(memory_space=pltpu.VMEM)] * 2,
        out_specs=pl.BlockSpec(memory_space=pltpu.VMEM),
        scratch_shapes=[
            pltpu.VMEM((n_z, tokens, width + half), bf16),
            pltpu.VMEM((n_z, 2 * tokens, width + half), bf16),
            pltpu.VMEM((half, width), f32),
            pltpu.VMEM((half, width), f32),
            pltpu.VMEM((n_long + 1, half, width), bf16),
            pltpu.VMEM((n_short + 1, half, width), bf16),
            pltpu.VMEM((width, width), bf16),
            pltpu.VMEM((width, width), f32),
            pltpu.VMEM((width, width), f32),
            pltpu.VMEM((width, width), bf16),
            pltpu.VMEM((width, width), f32),
            pltpu.VMEM((2, width, width), bf16),
            pltpu.VMEM((width, width), bf16),
            pltpu.VMEM((width, width), bf16),
            pltpu.VMEM((half, width), bf16),
            pltpu.VMEM((half, width), bf16),
            pieces,
            pieces,
            pieces,
            pieces,
            dma((n_z,)),
            dma((n_z,)),
            dma((n_long, CHUNKS)),
            dma((n_long, CHUNKS)),
            dma((n_short, CHUNKS)),
            dma((n_short, CHUNKS)),
            dma((CHUNKS,)),
            dma((CHUNKS,)),
            dma((STRIPS + 1,)),
            dma((STRIPS + 1,)),
            dma((n_x,)),
            dma((n_x,)),
            dma((n_x, n_y)),
            dma((n_x, n_y)),
        ],
        compiler_params=pltpu.CompilerParams(
            collective_id=0, has_side_effects=True, vmem_limit_bytes=40 * 1024 * 1024
        ),
    )(owners, block_shapes, acts, cotangents)


def solution(mesh):
    return jax.shard_map(
        functools.partial(local, mesh.shape["shard"], mesh.shape["rep"]),
        mesh=mesh,
        in_specs=(
            P("rep", "shard", None, None),
            P("rep", "shard", None, None),
            P("shard", None),
            P("shard"),
        ),
        out_specs=P(None, "rep", "shard", None),
        check_vma=False,
    )
```

```python
import functools
import math

import jax
import jax.numpy as jnp
from jax import lax
from jax.experimental import pallas as pl
from jax.experimental.pallas import tpu as pltpu
from jax.sharding import PartitionSpec as P

MESH = pl.DeviceIdType.MESH
DAMPING = 0.01
CHUNKS = 8
LOADS = 4
STRIPS = 4

ROWS_BY_ROWS = (((1,), (1,)), ((), ()))
COLUMNS_BY_COLUMNS = (((0,), (0,)), ((), ()))


def dot(a, b, dims=(((1,), (0,)), ((), ()))):
    return lax.dot_general(a, b, dims, preferred_element_type=jnp.float32)


def kernel(
    n_z, n_x, n_y,
    owners_hbm, shapes_hbm, acts_hbm, cots_hbm, out_ref,
    owners_ref, shapes_ref, acts_ref, cots_ref, staged, paired, part, ring, swapped, grad,
    stat, coupled, coupled_bf, work, work_bf, left, right,
    weighted, weighted_out, rows_own, rows_shift, rows_out,
    loaded, pair_send, pair_recv, ring_send, ring_recv,
    swap_send, swap_recv, root_send, root_recv, shift_send, shift_recv, rows_send, rows_recv,
):
    tokens, width = acts_ref.shape[1:]
    half = width // 2
    n_shard = n_x * n_y
    n_hops = n_z // 2
    shard = lax.axis_index("shard")
    rep = lax.axis_index("rep")
    z = rep // 2
    core = rep % 2
    x = shard // n_y
    y = shard % n_y
    sign = 1 - 2 * core
    partner = (shard, z * 2 + 1 - core)
    above = (shard, lax.rem(z + 1, n_z) * 2 + core)
    below = (shard, lax.rem(z + n_z - 1, n_z) * 2 + core)
    ring_to = (shard, lax.rem(z + sign + n_z, n_z) * 2 + core)

    def peer(across, along):
        return lax.rem(x + across, n_x) * n_y + lax.rem(y + along, n_y)

    span = n_z // LOADS
    loads = [
        pltpu.make_async_copy(owners_hbm, owners_ref, loaded.at[2 * LOADS]),
        pltpu.make_async_copy(shapes_hbm, shapes_ref, loaded.at[2 * LOADS + 1]),
    ]
    for index in range(LOADS):
        blocks = pl.ds(index * span, span)
        loads.append(pltpu.make_async_copy(cots_hbm.at[0, blocks], cots_ref.at[blocks], loaded.at[index]))
        loads.append(pltpu.make_async_copy(acts_hbm.at[0, blocks], acts_ref.at[blocks], loaded.at[LOADS + index]))
    for load in loads:
        load.start()

    barrier = pltpu.get_barrier_semaphore()
    for neighbour in (partner, above, below):
        pl.semaphore_signal(barrier, inc=1, device_id=neighbour, device_id_type=MESH)

    @pl.loop(1, n_shard)
    def _(step):
        to = (peer(step // n_y, lax.rem(step, n_y)), rep)
        pl.semaphore_signal(barrier, inc=1, device_id=to, device_id_type=MESH)

    for load in loads:
        load.wait()
    rotation = owners_ref[0]
    turn = lax.div(rotation, 2)
    parity = rotation - 2 * turn
    odd = parity.astype(jnp.float32)
    even = 1.0 - odd

    def block_of(chip):
        return lax.rem(chip + 2 * n_z - turn, n_z)

    def block_at(chip):
        return block_of(lax.rem(chip + n_z, n_z))

    own_tokens = pl.ds(pl.multiple_of(core * tokens, tokens), tokens)

    @pl.loop(0, n_hops + 1)
    def _(item):
        block = block_at(z - sign * (n_hops - item))
        staged[item, :, :width] = cots_ref[block]
        staged[item, :, width:] = acts_ref[block]

    def pair_copy(item):
        return pltpu.make_async_remote_copy(
            src_ref=staged.at[item],
            dst_ref=paired.at[item, own_tokens, :],
            send_sem=pair_send.at[item],
            recv_sem=pair_recv.at[item],
            device_id=partner,
            device_id_type=MESH,
        )

    pl.semaphore_wait(barrier, 3 + n_shard - 1)

    @pl.loop(0, n_hops + 1)
    def _(item):
        pair_copy(item).start()

    def partial(item):
        block = block_at(z + sign * (n_hops - item))
        paired[item, own_tokens, :width] = cots_ref[block]
        paired[item, own_tokens, width:] = acts_ref[block]
        pair_copy(item).wait_recv()
        return paired[item, :, :width]

    rows = width // CHUNKS
    few = CHUNKS // 2

    def span_of(chunk):
        return pl.ds(pl.multiple_of(chunk * rows, rows), rows)

    def ring_copy(step, chunk):
        return pltpu.make_async_remote_copy(
            src_ref=ring.at[step, span_of(chunk), :],
            dst_ref=ring.at[step + 1, span_of(chunk), :],
            send_sem=ring_send.at[step, chunk],
            recv_sem=ring_recv.at[step, chunk],
            device_id=ring_to,
            device_id_type=MESH,
        )

    outputs = partial(0)
    columns = pl.ds(pl.multiple_of(width + core * half, half), half)
    part[:half, :] = dot(paired[0, :, columns], outputs, COLUMNS_BY_COLUMNS)
    for chunk in range(few):
        ring[0, span_of(core * few + chunk), :] = part[chunk * rows : (chunk + 1) * rows, :].astype(jnp.bfloat16)
        ring_copy(0, core * few + chunk).start()

    def all_rows(item):
        outputs = partial(item)
        part[...] = dot(paired[item, :, width:], outputs, COLUMNS_BY_COLUMNS)

    def forward(step, chunk):
        span = span_of(chunk)
        ring_copy(step - 1, chunk).wait_recv()
        total = ring[step, span, :].astype(jnp.float32) + part[span, :]
        ring[step, span, :] = total.astype(jnp.bfloat16)
        ring_copy(step, chunk).start()

    all_rows(1)
    for chunk in range(few):
        place = (1 - core) * few + chunk
        ring[1, span_of(place), :] = part[span_of(place), :].astype(jnp.bfloat16)
        ring_copy(1, place).start()
    for chunk in range(few):
        forward(1, core * few + chunk)

    @pl.loop(2, n_hops)
    def _(step):
        all_rows(step)
        for chunk in range(CHUNKS):
            forward(step, chunk)

    all_rows(n_hops)

    own_block = block_of(z)
    live_rows = shapes_ref[0, own_block]
    live_columns = shapes_ref[1, own_block]

    def swap_copy(chunk):
        return pltpu.make_async_remote_copy(
            src_ref=ring.at[n_hops, span_of(chunk), :],
            dst_ref=swapped.at[span_of(chunk), :],
            send_sem=swap_send.at[chunk],
            recv_sem=swap_recv.at[chunk],
            device_id=partner,
            device_id_type=MESH,
        )

    def gather(chunk):
        span = slice(chunk * rows, (chunk + 1) * rows)
        swap_copy(chunk).wait_recv()
        total = ring[n_hops, span, :].astype(jnp.float32) + swapped[span, :].astype(jnp.float32)
        total = total + part[span, :]
        below_limit = live_rows - chunk * rows - lax.broadcasted_iota(jnp.int32, (rows, width), 0)
        before_limit = live_columns - lax.broadcasted_iota(jnp.int32, (rows, width), 1)
        live = jnp.minimum(jnp.maximum(jnp.minimum(below_limit, before_limit), 0), 1)
        grad[span, :] = (total * live.astype(jnp.float32)).astype(jnp.bfloat16)

    for chunk in range(CHUNKS):
        ring_copy(n_hops - 1, chunk).wait_recv()
        swap_copy(chunk).start()
        if chunk > 0:
            gather(chunk - 1)
    gather(CHUNKS - 1)

    deep = width // STRIPS
    strips = [slice(i * deep, (i + 1) * deep) for i in range(STRIPS)]

    @pl.when(core == 0)
    def _():
        for strip in strips:
            stat[strip, :] = dot(grad[strip, :], grad[...], ROWS_BY_ROWS)

    @pl.when(core == 1)
    def _():
        for strip in strips:
            stat[strip, :] = dot(grad[:, strip], grad[...], COLUMNS_BY_COLUMNS)

    def diagonal(strip):
        return (
            lax.broadcasted_iota(jnp.int32, (deep, width), 0) + strip.start
            == lax.broadcasted_iota(jnp.int32, (deep, width), 1)
        )

    squares = jnp.zeros((1, 1), jnp.float32)
    trace = jnp.zeros((1, 1), jnp.float32)
    for strip in strips:
        values = stat[strip, :]
        squares += jnp.sum(values * values, keepdims=True)
        trace += jnp.sum(jnp.where(diagonal(strip), values, 0.0), keepdims=True)
    damping = DAMPING * (trace / width + 1e-06)
    norm_squared = squares + damping * (2.0 * trace + width * damping)
    inverse = lax.rsqrt(norm_squared)
    scale = lax.rsqrt(jnp.sqrt(jnp.sqrt(norm_squared)))

    for strip in strips:
        values = (stat[strip, :] + jnp.where(diagonal(strip), damping, 0.0)) * inverse
        coupled[strip, :] = values
        coupled_bf[strip, :] = values.astype(jnp.bfloat16)
    for strip in strips:
        square = dot(coupled_bf[strip, :], coupled_bf[...])
        values = 0.0625 * square - 0.625 * coupled[strip, :]
        stat[strip, :] = values
        work_bf[0, strip, :] = values.astype(jnp.bfloat16)
    for strip in strips:
        square = dot(work_bf[0, strip, :], work_bf[0])
        work_bf[1, strip, :] = (square + 3.125 * stat[strip, :]).astype(jnp.bfloat16)
    for strip in strips:
        values = dot(work_bf[1, strip, :], coupled_bf[...]) + 2.44140625 * coupled[strip, :]
        work[strip, :] = values
        work_bf[0, strip, :] = values.astype(jnp.bfloat16)

    def root(strip):
        values = 0.0625 * dot(coupled_bf[strip, :], work_bf[0])
        values = values - 0.3125 * (coupled[strip, :] + work[strip, :])
        values = values + jnp.where(diagonal(strip), 1.5625, 0.0)
        return (values * scale).astype(jnp.bfloat16)

    def right_copy(index):
        span = pl.ds(index * deep, deep)
        return pltpu.make_async_remote_copy(
            src_ref=right.at[span, :],
            dst_ref=right.at[span, :],
            send_sem=root_send.at[index],
            recv_sem=root_recv.at[index],
            device_id=partner,
            device_id_type=MESH,
        )

    weighted_copy = pltpu.make_async_remote_copy(
        src_ref=weighted_out,
        dst_ref=weighted,
        send_sem=root_send.at[STRIPS],
        recv_sem=root_recv.at[STRIPS],
        device_id=partner,
        device_id_type=MESH,
    )

    @pl.when(core == 1)
    def _():
        for index, strip in enumerate(strips):
            right[strip, :] = root(strip)
            right_copy(index).start()
        weighted_copy.wait_recv()

    @pl.when(core == 0)
    def _():
        for index, strip in enumerate(strips):
            place = index % (STRIPS // 2) * deep
            left[index // (STRIPS // 2), place : place + deep, :] = root(strip)
        weighted_out[...] = dot(left[1 - parity], grad[...]).astype(jnp.bfloat16)
        weighted_copy.start()
        weighted[...] = dot(left[parity], grad[...]).astype(jnp.bfloat16)
        for index in range(STRIPS):
            right_copy(index).wait_recv()

    piece = half // n_shard
    spread = half // n_x

    def update_rows(into):
        for across in range(n_x):
            values = dot(weighted[across * spread : (across + 1) * spread, :], right[...]) * math.sqrt(width)
            values = values.reshape(n_y, piece, width)
            values = jnp.concatenate([values[:, :, :half], values[:, :, half:]], axis=1)
            into[:, across] = values.astype(jnp.bfloat16)

    far_first = sorted(range(n_y), key=lambda along: -min(along, n_y - along))
    far_first_x = sorted(range(n_x), key=lambda across: -min(across, n_x - across))

    def column(along):
        return lax.rem(y + along, n_y)

    def shift_copy(along):
        return pltpu.make_async_remote_copy(
            src_ref=rows_own.at[column(along)],
            dst_ref=rows_shift.at[column(along)],
            send_sem=shift_send.at[along],
            recv_sem=shift_recv.at[along],
            device_id=above,
            device_id_type=MESH,
        )

    def rows_copy(across, along):
        return pltpu.make_async_remote_copy(
            src_ref=rows_out.at[column(along), lax.rem(x + across, n_x)],
            dst_ref=out_ref.at[shard],
            send_sem=rows_send.at[across, along],
            recv_sem=rows_recv.at[across, along],
            device_id=(peer(across, along), rep),
            device_id_type=MESH,
        )

    own_copy = pltpu.make_async_copy(rows_out.at[y, x], out_ref.at[shard], rows_send.at[0, 0])

    def send_rows(along):
        for across in far_first_x:
            if (across, along) == (0, 0):
                own_copy.start()
            else:
                rows_copy(across, along).start()

    @pl.when(core == 1)
    def _():
        update_rows(rows_out)
        for along in far_first:
            send_rows(along)

    @pl.when(core == 0)
    def _():
        update_rows(rows_own)
        for along in far_first:
            shift_copy(along).start()
        for along in far_first:
            shift_copy(along).wait_recv()
            place = column(along)
            moved = rows_shift[place].astype(jnp.float32)
            values = moved * odd + rows_own[place].astype(jnp.float32) * even
            rows_out[place] = values.astype(jnp.bfloat16)
            send_rows(along)

    own_copy.wait()

    @pl.loop(1, n_shard)
    def _(step):
        rows_copy(step // n_y, lax.rem(step, n_y)).wait_recv()

    @pl.loop(0, n_hops + 1)
    def _(item):
        pair_copy(item).wait_send()

    for chunk in range(few):
        ring_copy(0, core * few + chunk).wait_send()

    @pl.loop(1, n_hops)
    def _(step):
        for chunk in range(CHUNKS):
            ring_copy(step, chunk).wait_send()

    for chunk in range(CHUNKS):
        swap_copy(chunk).wait_send()

    @pl.when(core == 1)
    def _():
        for index in range(STRIPS):
            right_copy(index).wait_send()

    @pl.when(core == 0)
    def _():
        weighted_copy.wait_send()
        for along in range(n_y):
            shift_copy(along).wait_send()

    for across in range(n_x):
        for along in range(n_y):
            if (across, along) != (0, 0):
                rows_copy(across, along).wait_send()


def local(n_shard, n_rep, acts, cotangents, block_shapes, owners):
    n_z = n_rep // 2
    n_x = 4 if n_shard == 32 else 1
    n_y = n_shard // n_x
    tokens, width = acts.shape[2:]
    half = width // 2
    n_hops = n_z // 2
    piece = half // n_shard
    bf16, f32 = jnp.bfloat16, jnp.float32
    dma = pltpu.SemaphoreType.DMA
    pieces = pltpu.VMEM((n_y, n_x, 2 * piece, half), bf16)
    rows = pl.pallas_call(
        functools.partial(kernel, n_z, n_x, n_y),
        out_shape=pltpu.VMEM((n_shard, 2 * piece, half), bf16),
        in_specs=[pl.BlockSpec(memory_space=pltpu.HBM)] * 4,
        out_specs=pl.BlockSpec(memory_space=pltpu.VMEM),
        scratch_shapes=[
            pltpu.SMEM(owners.shape, jnp.int32),
            pltpu.SMEM(block_shapes.shape[::-1], jnp.int32),
            pltpu.VMEM(acts.shape[1:], bf16),
            pltpu.VMEM(cotangents.shape[1:], bf16),
            pltpu.VMEM((n_hops + 1, tokens, 2 * width), bf16),
            pltpu.VMEM((n_hops + 1, 2 * tokens, 2 * width), bf16),
            pltpu.VMEM((width, width), f32),
            pltpu.VMEM((n_hops + 1, width, width), bf16),
            pltpu.VMEM((width, width), bf16),
            pltpu.VMEM((width, width), bf16),
            pltpu.VMEM((width, width), f32),
            pltpu.VMEM((width, width), f32),
            pltpu.VMEM((width, width), bf16),
            pltpu.VMEM((width, width), f32),
            pltpu.VMEM((2, width, width), bf16),
            pltpu.VMEM((2, half, width), bf16),
            pltpu.VMEM((width, width), bf16),
            pltpu.VMEM((half, width), bf16),
            pltpu.VMEM((half, width), bf16),
            pieces,
            pieces,
            pieces,
            dma((2 * LOADS + 2,)),
            dma((n_hops + 1,)),
            dma((n_hops + 1,)),
            dma((n_hops, CHUNKS)),
            dma((n_hops, CHUNKS)),
            dma((CHUNKS,)),
            dma((CHUNKS,)),
            dma((STRIPS + 1,)),
            dma((STRIPS + 1,)),
            dma((n_y,)),
            dma((n_y,)),
            dma((n_x, n_y)),
            dma((n_x, n_y)),
        ],
        compiler_params=pltpu.CompilerParams(
            collective_id=0, has_side_effects=True, vmem_limit_bytes=62 * 1024 * 1024
        ),
    )(owners, block_shapes.T, acts, cotangents)
    rows = rows.astype(f32).reshape(n_shard, 2, piece, half).transpose(0, 2, 1, 3)
    return rows.reshape(n_shard, 1, piece, width)


def solution(mesh):
    return jax.shard_map(
        functools.partial(local, mesh.shape["shard"], mesh.shape["rep"]),
        mesh=mesh,
        in_specs=(
            P("rep", "shard", None, None),
            P("rep", "shard", None, None),
            P("shard", None),
            P("shard"),
        ),
        out_specs=P(None, "rep", "shard", None),
        check_vma=False,
    )
```

```python
import functools
import math

import jax
import jax.numpy as jnp
from jax import lax
from jax.experimental import pallas as pl
from jax.experimental.pallas import tpu as pltpu
from jax.sharding import PartitionSpec as P

MESH = pl.DeviceIdType.MESH
DAMPING = 0.01
ROOT = [value / 4096.0 for value in (6400, -4405, 3125, -1250, 250, -25, 1)]
CHUNKS = 8
LOADS = 4
STRIPS = 2

ROWS_BY_ROWS = (((1,), (1,)), ((), ()))
COLUMNS_BY_COLUMNS = (((0,), (0,)), ((), ()))


def dot(a, b, dims=(((1,), (0,)), ((), ()))):
    return lax.dot_general(a, b, dims, preferred_element_type=jnp.float32)


def kernel(
    n_z, n_x, n_y,
    owners_hbm, shapes_hbm, acts_hbm, cots_hbm, out_ref,
    owners_ref, shapes_ref, acts_ref, cots_ref, staged, paired, part, ring, swapped, grad,
    stat, stat_bf, second, second_bf, third_bf, rest_bf, left, right,
    weighted, weighted_out, rows_own, rows_shift, rows_out,
    loaded, pair_send, pair_recv, ring_send, ring_recv,
    swap_send, swap_recv, root_send, root_recv, shift_send, shift_recv, rows_send, rows_recv, token,
):
    tokens, width = acts_ref.shape[1:]
    half = width // 2
    n_shard = n_x * n_y
    n_hops = n_z // 2
    shard = lax.axis_index("shard")
    rep = lax.axis_index("rep")
    z = rep // 2
    core = rep % 2
    x = shard // n_y
    y = shard % n_y
    sign = 1 - 2 * core
    partner = (shard, z * 2 + 1 - core)
    above = (shard, lax.rem(z + 1, n_z) * 2 + core)
    below = (shard, lax.rem(z + n_z - 1, n_z) * 2 + core)
    ring_to = (shard, lax.rem(z + sign + n_z, n_z) * 2 + core)

    def peer(across, along):
        return lax.rem(x + across, n_x) * n_y + lax.rem(y + along, n_y)

    span = n_z // LOADS
    loads = [
        pltpu.make_async_copy(owners_hbm, owners_ref, loaded.at[2 * LOADS]),
        pltpu.make_async_copy(shapes_hbm, shapes_ref, loaded.at[2 * LOADS + 1]),
    ]
    for index in range(LOADS):
        blocks = pl.ds(index * span, span)
        loads.append(pltpu.make_async_copy(cots_hbm.at[0, blocks], cots_ref.at[blocks], loaded.at[index]))
        loads.append(pltpu.make_async_copy(acts_hbm.at[0, blocks], acts_ref.at[blocks], loaded.at[LOADS + index]))
    for load in loads:
        load.start()

    barrier = pltpu.get_barrier_semaphore()
    neighbours = [partner, above, below, (peer(0, 1), rep), (peer(0, n_y - 1), rep)]
    if n_x > 1:
        neighbours += [(peer(1, 0), rep), (peer(n_x - 1, 0), rep)]
    for neighbour in neighbours:
        pl.semaphore_signal(barrier, inc=1, device_id=neighbour, device_id_type=MESH)

    rounds_y = n_y // 2 - 1
    rounds = rounds_y + n_x // 2

    def greet(turn):
        turn = jnp.int32(turn)
        along = jnp.minimum(jnp.maximum(rounds_y - turn, 0), 1)
        across = 1 - along
        for side, to in enumerate((peer(across, along), peer(n_x - across, n_y - along))):
            pl.semaphore_signal(token.at[turn, side], inc=1, device_id=(to, rep), device_id_type=MESH)

    def hear(turn):
        for side in range(2):
            pl.semaphore_wait(token.at[turn, side], 1)

    for load in loads:
        load.wait()
    rotation = owners_ref[0]
    turn = lax.div(rotation, 2)
    parity = rotation - 2 * turn
    odd = parity.astype(jnp.float32)
    even = 1.0 - odd

    def block_of(chip):
        return lax.rem(chip + 2 * n_z - turn, n_z)

    def block_at(chip):
        return block_of(lax.rem(chip + n_z, n_z))

    own_tokens = pl.ds(pl.multiple_of(core * tokens, tokens), tokens)

    def pair_copy(item):
        return pltpu.make_async_remote_copy(
            src_ref=staged.at[item],
            dst_ref=paired.at[item, own_tokens, :],
            send_sem=pair_send.at[item],
            recv_sem=pair_recv.at[item],
            device_id=partner,
            device_id_type=MESH,
        )

    pl.semaphore_wait(barrier, len(neighbours))

    @pl.loop(0, n_hops + 1)
    def _(item):
        block = block_at(z - sign * (n_hops - item))
        staged[item, :, :width] = cots_ref[block]
        staged[item, :, width:] = acts_ref[block]
        pair_copy(item).start()

    def partial(item):
        block = block_at(z + sign * (n_hops - item))
        paired[item, own_tokens, :width] = cots_ref[block]
        paired[item, own_tokens, width:] = acts_ref[block]
        pair_copy(item).wait_recv()
        return paired[item, :, :width]

    rows = width // CHUNKS
    few = CHUNKS // 2

    def span_of(chunk):
        return pl.ds(pl.multiple_of(chunk * rows, rows), rows)

    def ring_copy(step, chunk):
        return pltpu.make_async_remote_copy(
            src_ref=ring.at[step, span_of(chunk), :],
            dst_ref=ring.at[step + 1, span_of(chunk), :],
            send_sem=ring_send.at[step, chunk],
            recv_sem=ring_recv.at[step, chunk],
            device_id=ring_to,
            device_id_type=MESH,
        )

    outputs = partial(0)
    columns = pl.ds(pl.multiple_of(width + core * half, half), half)
    part[:half, :] = dot(paired[0, :, columns], outputs, COLUMNS_BY_COLUMNS)
    for chunk in range(few):
        ring[0, span_of(core * few + chunk), :] = part[chunk * rows : (chunk + 1) * rows, :].astype(jnp.bfloat16)
        ring_copy(0, core * few + chunk).start()

    greet(0)

    def all_rows(item):
        outputs = partial(item)
        part[...] = dot(paired[item, :, width:], outputs, COLUMNS_BY_COLUMNS)

    def forward(step, chunk):
        span = span_of(chunk)
        ring_copy(step - 1, chunk).wait_recv()
        total = ring[step, span, :].astype(jnp.float32) + part[span, :]
        ring[step, span, :] = total.astype(jnp.bfloat16)
        ring_copy(step, chunk).start()

    all_rows(1)
    for chunk in range(few):
        place = (1 - core) * few + chunk
        ring[1, span_of(place), :] = part[span_of(place), :].astype(jnp.bfloat16)
        ring_copy(1, place).start()
    for chunk in range(few):
        forward(1, core * few + chunk)

    hear(0)
    if rounds > 1:
        greet(1)

    @pl.loop(2, n_hops)
    def _(step):
        all_rows(step)
        for chunk in range(CHUNKS):
            forward(step, chunk)
        hear(step - 1)

        @pl.when(step < rounds)
        def _():
            greet(step)

    all_rows(n_hops)

    own_block = block_of(z)
    live_rows = shapes_ref[0, own_block]
    live_columns = shapes_ref[1, own_block]

    def swap_copy(chunk):
        return pltpu.make_async_remote_copy(
            src_ref=ring.at[n_hops, span_of(chunk), :],
            dst_ref=swapped.at[span_of(chunk), :],
            send_sem=swap_send.at[chunk],
            recv_sem=swap_recv.at[chunk],
            device_id=partner,
            device_id_type=MESH,
        )

    def gather(chunk):
        span = slice(chunk * rows, (chunk + 1) * rows)
        swap_copy(chunk).wait_recv()
        total = ring[n_hops, span, :].astype(jnp.float32) + swapped[span, :].astype(jnp.float32)
        total = total + part[span, :]
        below_limit = live_rows - chunk * rows - lax.broadcasted_iota(jnp.int32, (rows, width), 0)
        before_limit = live_columns - lax.broadcasted_iota(jnp.int32, (rows, width), 1)
        live = jnp.minimum(jnp.maximum(jnp.minimum(below_limit, before_limit), 0), 1)
        grad[span, :] = (total * live.astype(jnp.float32)).astype(jnp.bfloat16)

    for chunk in range(CHUNKS):
        ring_copy(n_hops - 1, chunk).wait_recv()
        swap_copy(chunk).start()
        if chunk > 0:
            gather(chunk - 1)
    gather(CHUNKS - 1)

    deep = width // STRIPS
    strips = [slice(i * deep, (i + 1) * deep) for i in range(STRIPS)]

    def keep(strip, values):
        stat[strip, :] = values
        stat_bf[strip, :] = values.astype(jnp.bfloat16)

    @pl.when(core == 0)
    def _():
        for strip in strips:
            keep(strip, dot(grad[strip, :], grad[...], ROWS_BY_ROWS))

    @pl.when(core == 1)
    def _():
        for strip in strips:
            keep(strip, dot(grad[:, strip], grad[...], COLUMNS_BY_COLUMNS))

    def diagonal(strip):
        return (
            lax.broadcasted_iota(jnp.int32, (deep, width), 0) + strip.start
            == lax.broadcasted_iota(jnp.int32, (deep, width), 1)
        )

    for strip in strips:
        second[strip, :] = dot(stat_bf[strip, :], stat_bf[...])
    squares = jnp.zeros((1, 1), jnp.float32)
    trace = jnp.zeros((1, 1), jnp.float32)
    for strip in strips:
        values = stat[strip, :]
        squares += jnp.sum(values * values, keepdims=True)
        trace += jnp.sum(jnp.where(diagonal(strip), values, 0.0), keepdims=True)
    damping = DAMPING * (trace / width + 1e-06)
    norm_squared = squares + damping * (2.0 * trace + width * damping)
    inverse = lax.rsqrt(norm_squared)
    scale = lax.rsqrt(jnp.sqrt(jnp.sqrt(norm_squared)))

    for strip in strips:
        eye = jnp.where(diagonal(strip), damping, 0.0)
        values = stat[strip, :]
        square = (second[strip, :] + damping * (2.0 * values + eye)) * inverse * inverse
        values = (values + eye) * inverse
        stat[strip, :] = values
        stat_bf[strip, :] = values.astype(jnp.bfloat16)
        second[strip, :] = square
        second_bf[strip, :] = square.astype(jnp.bfloat16)
    for strip in strips:
        cube = dot(second_bf[strip, :], stat_bf[...])
        third_bf[strip, :] = cube.astype(jnp.bfloat16)
        one, two = stat[strip, :], second[strip, :]
        rest_bf[strip, :] = (ROOT[4] * one + ROOT[5] * two + ROOT[6] * cube).astype(jnp.bfloat16)
        lead = ROOT[1] * one + ROOT[2] * two + ROOT[3] * cube
        second[strip, :] = lead + jnp.where(diagonal(strip), ROOT[0], 0.0)

    def root(strip):
        values = second[strip, :] + dot(third_bf[strip, :], rest_bf[...])
        return (values * scale).astype(jnp.bfloat16)

    def right_copy(index):
        span = pl.ds(index * deep, deep)
        return pltpu.make_async_remote_copy(
            src_ref=right.at[span, :],
            dst_ref=right.at[span, :],
            send_sem=root_send.at[index],
            recv_sem=root_recv.at[index],
            device_id=partner,
            device_id_type=MESH,
        )

    weighted_copy = pltpu.make_async_remote_copy(
        src_ref=weighted_out,
        dst_ref=weighted,
        send_sem=root_send.at[STRIPS],
        recv_sem=root_recv.at[STRIPS],
        device_id=partner,
        device_id_type=MESH,
    )

    @pl.when(core == 1)
    def _():
        for index, strip in enumerate(strips):
            right[strip, :] = root(strip)
            right_copy(index).start()
        weighted_copy.wait_recv()

    @pl.when(core == 0)
    def _():
        for index, strip in enumerate(strips):
            place = index % (STRIPS // 2) * deep
            left[index // (STRIPS // 2), place : place + deep, :] = root(strip)
        weighted_out[...] = dot(left[1 - parity], grad[...]).astype(jnp.bfloat16)
        weighted_copy.start()
        weighted[...] = dot(left[parity], grad[...]).astype(jnp.bfloat16)
        for index in range(STRIPS):
            right_copy(index).wait_recv()

    piece = half // n_shard

    def update_rows(into):
        values = dot(weighted[...], right[...]) * math.sqrt(width)
        values = values.reshape(n_x, n_y, piece, width)
        for across in range(n_x):
            folded = jnp.concatenate([values[across, :, :, :half], values[across, :, :, half:]], axis=1)
            into[:, across] = folded.astype(jnp.bfloat16)

    far_first = sorted(range(n_y), key=lambda along: -min(along, n_y - along))
    far_first_x = sorted(range(n_x), key=lambda across: -min(across, n_x - across))

    def column(along):
        return lax.rem(y + along, n_y)

    def shift_copy(along):
        return pltpu.make_async_remote_copy(
            src_ref=rows_own.at[column(along)],
            dst_ref=rows_shift.at[column(along)],
            send_sem=shift_send.at[along],
            recv_sem=shift_recv.at[along],
            device_id=above,
            device_id_type=MESH,
        )

    def rows_copy(across, along):
        return pltpu.make_async_remote_copy(
            src_ref=rows_out.at[column(along), lax.rem(x + across, n_x)],
            dst_ref=out_ref.at[shard],
            send_sem=rows_send.at[across, along],
            recv_sem=rows_recv.at[across, along],
            device_id=(peer(across, along), rep),
            device_id_type=MESH,
        )

    own_copy = pltpu.make_async_copy(rows_out.at[y, x], out_ref.at[shard], rows_send.at[0, 0])

    def send_rows(along):
        for across in far_first_x:
            if (across, along) == (0, 0):
                own_copy.start()
            else:
                rows_copy(across, along).start()

    @pl.when(core == 1)
    def _():
        update_rows(rows_out)
        for along in far_first:
            send_rows(along)

    @pl.when(core == 0)
    def _():
        update_rows(rows_own)
        for along in far_first:
            shift_copy(along).start()
        for along in far_first:
            shift_copy(along).wait_recv()
            place = column(along)
            moved = rows_shift[place].astype(jnp.float32)
            values = moved * odd + rows_own[place].astype(jnp.float32) * even
            rows_out[place] = values.astype(jnp.bfloat16)
            send_rows(along)

    own_copy.wait()

    @pl.loop(1, n_shard)
    def _(step):
        rows_copy(step // n_y, lax.rem(step, n_y)).wait_recv()

    @pl.loop(0, n_hops + 1)
    def _(item):
        pair_copy(item).wait_send()

    for chunk in range(few):
        ring_copy(0, core * few + chunk).wait_send()

    @pl.loop(1, n_hops)
    def _(step):
        for chunk in range(CHUNKS):
            ring_copy(step, chunk).wait_send()

    for chunk in range(CHUNKS):
        swap_copy(chunk).wait_send()

    @pl.when(core == 1)
    def _():
        for index in range(STRIPS):
            right_copy(index).wait_send()

    @pl.when(core == 0)
    def _():
        weighted_copy.wait_send()
        for along in range(n_y):
            shift_copy(along).wait_send()

    for across in range(n_x):
        for along in range(n_y):
            if (across, along) != (0, 0):
                rows_copy(across, along).wait_send()


def local(n_shard, n_rep, acts, cotangents, block_shapes, owners):
    n_z = n_rep // 2
    n_x = 4 if n_shard == 32 else 1
    n_y = n_shard // n_x
    tokens, width = acts.shape[2:]
    half = width // 2
    n_hops = n_z // 2
    piece = half // n_shard
    bf16, f32 = jnp.bfloat16, jnp.float32
    dma = pltpu.SemaphoreType.DMA
    pieces = pltpu.VMEM((n_y, n_x, 2 * piece, half), bf16)
    rows = pl.pallas_call(
        functools.partial(kernel, n_z, n_x, n_y),
        out_shape=pltpu.VMEM((n_shard, 2 * piece, half), bf16),
        in_specs=[pl.BlockSpec(memory_space=pltpu.HBM)] * 4,
        out_specs=pl.BlockSpec(memory_space=pltpu.VMEM),
        scratch_shapes=[
            pltpu.SMEM(owners.shape, jnp.int32),
            pltpu.SMEM(block_shapes.shape[::-1], jnp.int32),
            pltpu.VMEM(acts.shape[1:], bf16),
            pltpu.VMEM(cotangents.shape[1:], bf16),
            pltpu.VMEM((n_hops + 1, tokens, 2 * width), bf16),
            pltpu.VMEM((n_hops + 1, 2 * tokens, 2 * width), bf16),
            pltpu.VMEM((width, width), f32),
            pltpu.VMEM((n_hops + 1, width, width), bf16),
            pltpu.VMEM((width, width), bf16),
            pltpu.VMEM((width, width), bf16),
            pltpu.VMEM((width, width), f32),
            pltpu.VMEM((width, width), bf16),
            pltpu.VMEM((width, width), f32),
            pltpu.VMEM((width, width), bf16),
            pltpu.VMEM((width, width), bf16),
            pltpu.VMEM((width, width), bf16),
            pltpu.VMEM((2, half, width), bf16),
            pltpu.VMEM((width, width), bf16),
            pltpu.VMEM((half, width), bf16),
            pltpu.VMEM((half, width), bf16),
            pieces,
            pieces,
            pieces,
            dma((2 * LOADS + 2,)),
            dma((n_hops + 1,)),
            dma((n_hops + 1,)),
            dma((n_hops, CHUNKS)),
            dma((n_hops, CHUNKS)),
            dma((CHUNKS,)),
            dma((CHUNKS,)),
            dma((STRIPS + 1,)),
            dma((STRIPS + 1,)),
            dma((n_y,)),
            dma((n_y,)),
            dma((n_x, n_y)),
            dma((n_x, n_y)),
            pltpu.SemaphoreType.REGULAR((n_z // 2 - 1, 2)),
        ],
        compiler_params=pltpu.CompilerParams(
            collective_id=0, has_side_effects=True, vmem_limit_bytes=62 * 1024 * 1024
        ),
    )(owners, block_shapes.T, acts, cotangents)
    rows = rows.astype(f32).reshape(n_shard, 2, piece, half).transpose(0, 2, 1, 3)
    return rows.reshape(n_shard, 1, piece, width)


def solution(mesh):
    return jax.shard_map(
        functools.partial(local, mesh.shape["shard"], mesh.shape["rep"]),
        mesh=mesh,
        in_specs=(
            P("rep", "shard", None, None),
            P("rep", "shard", None, None),
            P("shard", None),
            P("shard"),
        ),
        out_specs=P(None, "rep", "shard", None),
        check_vma=False,
    )
```

```python
import functools
import math

import jax
import jax.numpy as jnp
from jax import lax
from jax.experimental import pallas as pl
from jax.experimental.pallas import tpu as pltpu
from jax.sharding import PartitionSpec as P

MESH = pl.DeviceIdType.MESH
DAMPING = 0.01
ROOT = [value / 4096.0 for value in (6400, -4405, 3125, -1250, 250, -25, 1)]
CHUNKS = 4
LOADS = 1
STRIPS = 2

ROWS_BY_ROWS = (((1,), (1,)), ((), ()))
COLUMNS_BY_COLUMNS = (((0,), (0,)), ((), ()))


def dot(a, b, dims=(((1,), (0,)), ((), ()))):
    return lax.dot_general(a, b, dims, preferred_element_type=jnp.float32)


def kernel(
    n_z, n_x, n_y,
    owners_hbm, shapes_hbm, acts_hbm, cots_hbm, out_ref,
    owners_ref, shapes_ref, acts_ref, cots_ref, staged, paired, part, ring, swapped, grad,
    stat, stat_bf, second, second_bf, third_bf, rest_bf, left, right,
    weighted, weighted_out, rows_own, rows_shift, rows_out,
    pool, pair_recv, ring_recv, swap_recv, root_send, root_recv, shift_send, shift_recv, rows_recv, token,
):
    tokens, width = acts_ref.shape[1:]
    half = width // 2
    n_shard = n_x * n_y
    n_hops = n_z // 2
    shard = lax.axis_index("shard")
    rep = lax.axis_index("rep")
    z = rep // 2
    core = rep % 2
    x = shard // n_y
    y = shard % n_y
    sign = 1 - 2 * core
    partner = (shard, z * 2 + 1 - core)
    above = (shard, lax.rem(z + 1, n_z) * 2 + core)
    below = (shard, lax.rem(z + n_z - 1, n_z) * 2 + core)
    ring_to = (shard, lax.rem(z + sign + n_z, n_z) * 2 + core)

    def peer(across, along):
        return lax.rem(x + across, n_x) * n_y + lax.rem(y + along, n_y)

    span = n_z // LOADS
    loads = [
        pltpu.make_async_copy(owners_hbm, owners_ref, pool.at[2 * LOADS]),
        pltpu.make_async_copy(shapes_hbm, shapes_ref, pool.at[2 * LOADS + 1]),
    ]
    for index in range(LOADS):
        blocks = pl.ds(index * span, span)
        loads.append(pltpu.make_async_copy(cots_hbm.at[0, blocks], cots_ref.at[blocks], pool.at[index]))
        loads.append(pltpu.make_async_copy(acts_hbm.at[0, blocks], acts_ref.at[blocks], pool.at[LOADS + index]))
    for load in loads:
        load.start()

    barrier = pltpu.get_barrier_semaphore()
    neighbours = [partner, above, below, (peer(0, 1), rep), (peer(0, n_y - 1), rep)]
    if n_x > 1:
        neighbours += [(peer(1, 0), rep), (peer(n_x - 1, 0), rep)]
    for neighbour in neighbours:
        pl.semaphore_signal(barrier, inc=1, device_id=neighbour, device_id_type=MESH)

    rounds_y = n_y // 2 - 1
    rounds = rounds_y + n_x // 2

    def greet(turn):
        turn = jnp.int32(turn)
        along = jnp.minimum(jnp.maximum(rounds_y - turn, 0), 1)
        across = 1 - along
        for side, to in enumerate((peer(across, along), peer(n_x - across, n_y - along))):
            pl.semaphore_signal(token.at[turn, side], inc=1, device_id=(to, rep), device_id_type=MESH)

    def hear(turn):
        for side in range(2):
            pl.semaphore_wait(token.at[turn, side], 1)

    for load in loads:
        load.wait()
    rotation = owners_ref[0]
    turn = lax.div(rotation, 2)
    parity = rotation - 2 * turn
    odd = parity.astype(jnp.float32)
    even = 1.0 - odd

    def block_of(chip):
        return lax.rem(chip + 2 * n_z - turn, n_z)

    def block_at(chip):
        return block_of(lax.rem(chip + n_z, n_z))

    own_tokens = pl.ds(pl.multiple_of(core * tokens, tokens), tokens)

    def pair_copy(item):
        return pltpu.make_async_remote_copy(
            src_ref=staged.at[item],
            dst_ref=paired.at[item, own_tokens, :],
            send_sem=shift_send.at[item],
            recv_sem=pair_recv.at[item],
            device_id=partner,
            device_id_type=MESH,
        )

    pl.semaphore_wait(barrier, len(neighbours))

    @pl.loop(0, n_hops + 1)
    def _(item):
        block = block_at(z - sign * (n_hops - item))
        staged[item, :, :width] = cots_ref[block]
        staged[item, :, width:] = acts_ref[block]
        pair_copy(item).start()

    def partial(item):
        block = block_at(z + sign * (n_hops - item))
        paired[item, own_tokens, :width] = cots_ref[block]
        paired[item, own_tokens, width:] = acts_ref[block]
        pair_copy(item).wait_recv()
        return paired[item, :, :width]

    rows = width // CHUNKS
    few = CHUNKS // 2

    def span_of(chunk):
        return pl.ds(pl.multiple_of(chunk * rows, rows), rows)

    def ring_copy(step, chunk):
        return pltpu.make_async_remote_copy(
            src_ref=ring.at[step, span_of(chunk), :],
            dst_ref=ring.at[step + 1, span_of(chunk), :],
            send_sem=pool.at[step * CHUNKS + chunk],
            recv_sem=ring_recv.at[step, chunk],
            device_id=ring_to,
            device_id_type=MESH,
        )

    outputs = partial(0)
    columns = pl.ds(pl.multiple_of(width + core * half, half), half)
    part[:half, :] = dot(paired[0, :, columns], outputs, COLUMNS_BY_COLUMNS)
    for chunk in range(few):
        ring[0, span_of(core * few + chunk), :] = part[chunk * rows : (chunk + 1) * rows, :].astype(jnp.bfloat16)
        ring_copy(0, core * few + chunk).start()

    greet(0)

    def all_rows(item):
        outputs = partial(item)
        part[...] = dot(paired[item, :, width:], outputs, COLUMNS_BY_COLUMNS)

    def forward(step, chunk):
        span = span_of(chunk)
        ring_copy(step - 1, chunk).wait_recv()
        total = ring[step, span, :].astype(jnp.float32) + part[span, :]
        ring[step, span, :] = total.astype(jnp.bfloat16)
        ring_copy(step, chunk).start()

    all_rows(1)
    for chunk in range(few):
        place = (1 - core) * few + chunk
        ring[1, span_of(place), :] = part[span_of(place), :].astype(jnp.bfloat16)
        ring_copy(1, place).start()
    for chunk in range(few):
        forward(1, core * few + chunk)

    hear(0)
    if rounds > 1:
        greet(1)

    @pl.loop(2, n_hops)
    def _(step):
        all_rows(step)
        for chunk in range(CHUNKS):
            forward(step, chunk)
        hear(step - 1)

        @pl.when(step < rounds)
        def _():
            greet(step)

    all_rows(n_hops)

    own_block = block_of(z)
    live_rows = shapes_ref[0, own_block]
    live_columns = shapes_ref[1, own_block]

    def swap_copy(chunk):
        return pltpu.make_async_remote_copy(
            src_ref=ring.at[n_hops, span_of(chunk), :],
            dst_ref=swapped.at[span_of(chunk), :],
            send_sem=pool.at[n_hops * CHUNKS + chunk],
            recv_sem=swap_recv.at[chunk],
            device_id=partner,
            device_id_type=MESH,
        )

    def gather(chunk):
        span = slice(chunk * rows, (chunk + 1) * rows)
        swap_copy(chunk).wait_recv()
        total = ring[n_hops, span, :].astype(jnp.float32) + swapped[span, :].astype(jnp.float32)
        total = total + part[span, :]
        below_limit = live_rows - chunk * rows - lax.broadcasted_iota(jnp.int32, (rows, width), 0)
        before_limit = live_columns - lax.broadcasted_iota(jnp.int32, (rows, width), 1)
        live = jnp.minimum(jnp.maximum(jnp.minimum(below_limit, before_limit), 0), 1)
        grad[span, :] = (total * live.astype(jnp.float32)).astype(jnp.bfloat16)

    for chunk in range(CHUNKS):
        ring_copy(n_hops - 1, chunk).wait_recv()
        swap_copy(chunk).start()
        if chunk > 0:
            gather(chunk - 1)
    gather(CHUNKS - 1)

    deep = width // STRIPS
    strips = [slice(i * deep, (i + 1) * deep) for i in range(STRIPS)]

    def keep(strip, values):
        stat[strip, :] = values
        stat_bf[strip, :] = values.astype(jnp.bfloat16)

    @pl.when(core == 0)
    def _():
        for strip in strips:
            keep(strip, dot(grad[strip, :], grad[...], ROWS_BY_ROWS))

    @pl.when(core == 1)
    def _():
        for strip in strips:
            keep(strip, dot(grad[:, strip], grad[...], COLUMNS_BY_COLUMNS))

    def diagonal(strip):
        return (
            lax.broadcasted_iota(jnp.int32, (deep, width), 0) + strip.start
            == lax.broadcasted_iota(jnp.int32, (deep, width), 1)
        )

    for strip in strips:
        second[strip, :] = dot(stat_bf[strip, :], stat_bf[...])
    squares = jnp.zeros((1, 1), jnp.float32)
    trace = jnp.zeros((1, 1), jnp.float32)
    for strip in strips:
        values = stat[strip, :]
        squares += jnp.sum(values * values, keepdims=True)
        trace += jnp.sum(jnp.where(diagonal(strip), values, 0.0), keepdims=True)
    damping = DAMPING * (trace / width + 1e-06)
    norm_squared = squares + damping * (2.0 * trace + width * damping)
    inverse = lax.rsqrt(norm_squared)
    scale = lax.rsqrt(jnp.sqrt(jnp.sqrt(norm_squared)))

    for strip in strips:
        eye = jnp.where(diagonal(strip), damping, 0.0)
        values = stat[strip, :]
        square = (second[strip, :] + damping * (2.0 * values + eye)) * inverse * inverse
        values = (values + eye) * inverse
        stat[strip, :] = values
        stat_bf[strip, :] = values.astype(jnp.bfloat16)
        second[strip, :] = square
        second_bf[strip, :] = square.astype(jnp.bfloat16)
    for strip in strips:
        cube = dot(second_bf[strip, :], stat_bf[...])
        third_bf[strip, :] = cube.astype(jnp.bfloat16)
        one, two = stat[strip, :], second[strip, :]
        rest_bf[strip, :] = (ROOT[4] * one + ROOT[5] * two + ROOT[6] * cube).astype(jnp.bfloat16)
        lead = ROOT[1] * one + ROOT[2] * two + ROOT[3] * cube
        second[strip, :] = lead + jnp.where(diagonal(strip), ROOT[0], 0.0)

    def root(strip):
        values = second[strip, :] + dot(third_bf[strip, :], rest_bf[...])
        return (values * scale).astype(jnp.bfloat16)

    def right_copy(index):
        span = pl.ds(index * deep, deep)
        return pltpu.make_async_remote_copy(
            src_ref=right.at[span, :],
            dst_ref=right.at[span, :],
            send_sem=root_send.at[index],
            recv_sem=root_recv.at[index],
            device_id=partner,
            device_id_type=MESH,
        )

    weighted_copy = pltpu.make_async_remote_copy(
        src_ref=weighted_out,
        dst_ref=weighted,
        send_sem=root_send.at[STRIPS],
        recv_sem=root_recv.at[STRIPS],
        device_id=partner,
        device_id_type=MESH,
    )

    @pl.when(core == 1)
    def _():
        for index, strip in enumerate(strips):
            right[strip, :] = root(strip)
            right_copy(index).start()
        weighted_copy.wait_recv()

    @pl.when(core == 0)
    def _():
        for index, strip in enumerate(strips):
            place = index % (STRIPS // 2) * deep
            left[index // (STRIPS // 2), place : place + deep, :] = root(strip)
        weighted_out[...] = dot(left[1 - parity], grad[...]).astype(jnp.bfloat16)
        weighted_copy.start()
        weighted[...] = dot(left[parity], grad[...]).astype(jnp.bfloat16)
        for index in range(STRIPS):
            right_copy(index).wait_recv()

    @pl.loop(0, n_hops + 1)
    def _(item):
        pair_copy(item).wait_send()

    for chunk in range(few):
        ring_copy(0, core * few + chunk).wait_send()

    @pl.loop(1, n_hops)
    def _(step):
        for chunk in range(CHUNKS):
            ring_copy(step, chunk).wait_send()

    for chunk in range(CHUNKS):
        swap_copy(chunk).wait_send()

    piece = half // n_shard

    def update_rows(into):
        values = dot(weighted[...], right[...]) * math.sqrt(width)
        values = values.reshape(n_x, n_y, piece, width)
        for across in range(n_x):
            folded = jnp.concatenate([values[across, :, :, :half], values[across, :, :, half:]], axis=1)
            into[:, across] = folded.astype(jnp.bfloat16)

    far_first = sorted(range(n_y), key=lambda along: -min(along, n_y - along))
    far_first_x = sorted(range(n_x), key=lambda across: -min(across, n_x - across))

    def column(along):
        return lax.rem(y + along, n_y)

    def shift_copy(along):
        return pltpu.make_async_remote_copy(
            src_ref=rows_own.at[column(along)],
            dst_ref=rows_shift.at[column(along)],
            send_sem=shift_send.at[along],
            recv_sem=shift_recv.at[along],
            device_id=above,
            device_id_type=MESH,
        )

    def rows_copy(across, along):
        return pltpu.make_async_remote_copy(
            src_ref=rows_out.at[column(along), lax.rem(x + across, n_x)],
            dst_ref=out_ref.at[shard],
            send_sem=pool.at[across * n_y + along],
            recv_sem=rows_recv.at[across, along],
            device_id=(peer(across, along), rep),
            device_id_type=MESH,
        )

    own_copy = pltpu.make_async_copy(rows_out.at[y, x], out_ref.at[shard], pool.at[0])

    def send_rows(along):
        for across in far_first_x:
            if (across, along) == (0, 0):
                own_copy.start()
            else:
                rows_copy(across, along).start()

    @pl.when(core == 1)
    def _():
        update_rows(rows_out)
        for along in far_first:
            send_rows(along)

    @pl.when(core == 0)
    def _():
        update_rows(rows_own)
        for along in far_first:
            shift_copy(along).start()
        for along in far_first:
            shift_copy(along).wait_recv()
            place = column(along)
            moved = rows_shift[place].astype(jnp.float32)
            values = moved * odd + rows_own[place].astype(jnp.float32) * even
            rows_out[place] = values.astype(jnp.bfloat16)
            send_rows(along)

    own_copy.wait()

    @pl.loop(1, n_shard)
    def _(step):
        rows_copy(step // n_y, lax.rem(step, n_y)).wait_recv()

    @pl.when(core == 1)
    def _():
        for index in range(STRIPS):
            right_copy(index).wait_send()

    @pl.when(core == 0)
    def _():
        weighted_copy.wait_send()
        for along in range(n_y):
            shift_copy(along).wait_send()

    for across in range(n_x):
        for along in range(n_y):
            if (across, along) != (0, 0):
                rows_copy(across, along).wait_send()


def local(n_shard, n_rep, acts, cotangents, block_shapes, owners):
    n_z = n_rep // 2
    n_x = 4 if n_shard == 32 else 1
    n_y = n_shard // n_x
    tokens, width = acts.shape[2:]
    half = width // 2
    n_hops = n_z // 2
    piece = half // n_shard
    bf16, f32 = jnp.bfloat16, jnp.float32
    dma = pltpu.SemaphoreType.DMA
    pieces = pltpu.VMEM((n_y, n_x, 2 * piece, half), bf16)
    rows = pl.pallas_call(
        functools.partial(kernel, n_z, n_x, n_y),
        out_shape=pltpu.VMEM((n_shard, 2 * piece, half), bf16),
        in_specs=[pl.BlockSpec(memory_space=pltpu.HBM)] * 4,
        out_specs=pl.BlockSpec(memory_space=pltpu.VMEM),
        scratch_shapes=[
            pltpu.SMEM(owners.shape, jnp.int32),
            pltpu.SMEM(block_shapes.shape[::-1], jnp.int32),
            pltpu.VMEM(acts.shape[1:], bf16),
            pltpu.VMEM(cotangents.shape[1:], bf16),
            pltpu.VMEM((n_hops + 1, tokens, 2 * width), bf16),
            pltpu.VMEM((n_hops + 1, 2 * tokens, 2 * width), bf16),
            pltpu.VMEM((width, width), f32),
            pltpu.VMEM((n_hops + 1, width, width), bf16),
            pltpu.VMEM((width, width), bf16),
            pltpu.VMEM((width, width), bf16),
            pltpu.VMEM((width, width), f32),
            pltpu.VMEM((width, width), bf16),
            pltpu.VMEM((width, width), f32),
            pltpu.VMEM((width, width), bf16),
            pltpu.VMEM((width, width), bf16),
            pltpu.VMEM((width, width), bf16),
            pltpu.VMEM((2, half, width), bf16),
            pltpu.VMEM((width, width), bf16),
            pltpu.VMEM((half, width), bf16),
            pltpu.VMEM((half, width), bf16),
            pieces,
            pieces,
            pieces,
            dma((max(n_shard, (n_hops + 1) * CHUNKS),)),
            dma((n_hops + 1,)),
            dma((n_hops, CHUNKS)),
            dma((CHUNKS,)),
            dma((STRIPS + 1,)),
            dma((STRIPS + 1,)),
            dma((max(n_y, n_hops + 1),)),
            dma((n_y,)),
            dma((n_x, n_y)),
            pltpu.SemaphoreType.REGULAR((n_z // 2 - 1, 2)),
        ],
        compiler_params=pltpu.CompilerParams(
            collective_id=0, has_side_effects=True, vmem_limit_bytes=62 * 1024 * 1024
        ),
    )(owners, block_shapes.T, acts, cotangents)
    rows = rows.astype(f32).reshape(n_shard, 2, piece, half).transpose(0, 2, 1, 3)
    return rows.reshape(n_shard, 1, piece, width)


def solution(mesh):
    return jax.shard_map(
        functools.partial(local, mesh.shape["shard"], mesh.shape["rep"]),
        mesh=mesh,
        in_specs=(
            P("rep", "shard", None, None),
            P("rep", "shard", None, None),
            P("shard", None),
            P("shard"),
        ),
        out_specs=P(None, "rep", "shard", None),
        check_vma=False,
    )
```

```python
import functools
import math

import jax
import jax.numpy as jnp
from jax import lax
from jax.experimental import pallas as pl
from jax.experimental.pallas import tpu as pltpu
from jax.sharding import PartitionSpec as P

MESH = pl.DeviceIdType.MESH
DAMPING = 0.01
ROOT = [value / 4096.0 for value in (6400, -4405, 3125, -1250, 250, -25, 1)]
CHUNKS = 4
LOADS = 1
STRIPS = 2

ROWS_BY_ROWS = (((1,), (1,)), ((), ()))
COLUMNS_BY_COLUMNS = (((0,), (0,)), ((), ()))


def dot(a, b, dims=(((1,), (0,)), ((), ()))):
    return lax.dot_general(a, b, dims, preferred_element_type=jnp.float32)


def kernel(
    n_z, n_x, n_y,
    owners_hbm, shapes_hbm, acts_hbm, cots_hbm, out_ref,
    owners_ref, shapes_ref, acts_ref, cots_ref, staged, paired, part, ring, swapped, grad,
    stat, stat_bf, second, second_bf, third_bf, rest_bf, left, right,
    weighted, weighted_out, rows_own, rows_shift, rows_out,
    pool, pair_recv, ring_recv, swap_recv, root_send, root_recv, shift_send, shift_recv, rows_recv, token,
):
    tokens, width = acts_ref.shape[1:]
    half = width // 2
    n_shard = n_x * n_y
    n_hops = n_z // 2
    shard = lax.axis_index("shard")
    rep = lax.axis_index("rep")
    z = rep // 2
    core = rep % 2
    x = shard // n_y
    y = shard % n_y
    sign = 1 - 2 * core
    partner = (shard, z * 2 + 1 - core)
    above = (shard, lax.rem(z + 1, n_z) * 2 + core)
    below = (shard, lax.rem(z + n_z - 1, n_z) * 2 + core)
    ring_to = (shard, lax.rem(z + sign + n_z, n_z) * 2 + core)

    def peer(across, along):
        return lax.rem(x + across, n_x) * n_y + lax.rem(y + along, n_y)

    span = n_z // LOADS
    loads = [
        pltpu.make_async_copy(owners_hbm, owners_ref, pool.at[2 * LOADS]),
        pltpu.make_async_copy(shapes_hbm, shapes_ref, pool.at[2 * LOADS + 1]),
    ]
    for index in range(LOADS):
        blocks = pl.ds(index * span, span)
        loads.append(pltpu.make_async_copy(cots_hbm.at[0, blocks], cots_ref.at[blocks], pool.at[index]))
        loads.append(pltpu.make_async_copy(acts_hbm.at[0, blocks], acts_ref.at[blocks], pool.at[LOADS + index]))
    for load in loads:
        load.start()

    barrier = pltpu.get_barrier_semaphore()
    neighbours = [partner, above, below, (peer(0, 1), rep), (peer(0, n_y - 1), rep)]
    if n_x > 1:
        neighbours += [(peer(1, 0), rep), (peer(n_x - 1, 0), rep)]
    for neighbour in neighbours:
        pl.semaphore_signal(barrier, inc=1, device_id=neighbour, device_id_type=MESH)

    rounds_y = n_y // 2 - 1
    rounds = rounds_y + n_x // 2

    def greet(turn):
        turn = jnp.int32(turn)
        along = jnp.minimum(jnp.maximum(rounds_y - turn, 0), 1)
        across = 1 - along
        for side, to in enumerate((peer(across, along), peer(n_x - across, n_y - along))):
            pl.semaphore_signal(token.at[turn, side], inc=1, device_id=(to, rep), device_id_type=MESH)

    def hear(turn):
        for side in range(2):
            pl.semaphore_wait(token.at[turn, side], 1)

    for load in loads:
        load.wait()
    rotation = owners_ref[0]
    turn = lax.div(rotation, 2)
    parity = rotation - 2 * turn
    odd = parity.astype(jnp.float32)
    even = 1.0 - odd

    def block_of(chip):
        return lax.rem(chip + 2 * n_z - turn, n_z)

    def block_at(chip):
        return block_of(lax.rem(chip + n_z, n_z))

    own_tokens = pl.ds(pl.multiple_of(core * tokens, tokens), tokens)

    def pair_copy(item):
        return pltpu.make_async_remote_copy(
            src_ref=staged.at[item],
            dst_ref=paired.at[item, own_tokens, :],
            send_sem=shift_send.at[item],
            recv_sem=pair_recv.at[item],
            device_id=partner,
            device_id_type=MESH,
        )

    pl.semaphore_wait(barrier, len(neighbours))

    @pl.loop(0, n_hops + 1)
    def _(item):
        block = block_at(z - sign * (n_hops - item))
        staged[item, :, :width] = cots_ref[block]
        staged[item, :, width:] = acts_ref[block]
        pair_copy(item).start()

    def partial(item):
        block = block_at(z + sign * (n_hops - item))
        paired[item, own_tokens, :width] = cots_ref[block]
        paired[item, own_tokens, width:] = acts_ref[block]
        pair_copy(item).wait_recv()
        return paired[item, :, :width]

    rows = width // CHUNKS
    few = CHUNKS // 2

    def span_of(chunk):
        return pl.ds(pl.multiple_of(chunk * rows, rows), rows)

    def ring_copy(step, chunk):
        return pltpu.make_async_remote_copy(
            src_ref=ring.at[step, span_of(chunk), :],
            dst_ref=ring.at[step + 1, span_of(chunk), :],
            send_sem=pool.at[step * CHUNKS + chunk],
            recv_sem=ring_recv.at[step, chunk],
            device_id=ring_to,
            device_id_type=MESH,
        )

    outputs = partial(0)
    columns = pl.ds(pl.multiple_of(width + core * half, half), half)
    part[:half, :] = dot(paired[0, :, columns], outputs, COLUMNS_BY_COLUMNS)
    for chunk in range(few):
        ring[0, span_of(core * few + chunk), :] = part[chunk * rows : (chunk + 1) * rows, :].astype(jnp.bfloat16)
        ring_copy(0, core * few + chunk).start()

    greet(0)

    def all_rows(item):
        outputs = partial(item)
        part[...] = dot(paired[item, :, width:], outputs, COLUMNS_BY_COLUMNS)

    def forward(step, chunk):
        span = span_of(chunk)
        ring_copy(step - 1, chunk).wait_recv()
        total = ring[step, span, :].astype(jnp.float32) + part[span, :]
        ring[step, span, :] = total.astype(jnp.bfloat16)
        ring_copy(step, chunk).start()

    all_rows(1)
    for chunk in range(few):
        place = (1 - core) * few + chunk
        ring[1, span_of(place), :] = part[span_of(place), :].astype(jnp.bfloat16)
        ring_copy(1, place).start()
    for chunk in range(few):
        forward(1, core * few + chunk)

    hear(0)
    if rounds > 1:
        greet(1)

    @pl.loop(2, n_hops)
    def _(step):
        all_rows(step)
        for chunk in range(CHUNKS):
            forward(step, chunk)
        hear(step - 1)

        @pl.when(step < rounds)
        def _():
            greet(step)

    all_rows(n_hops)

    own_block = block_of(z)
    live_rows = shapes_ref[0, own_block]
    live_columns = shapes_ref[1, own_block]

    def swap_copy(chunk):
        return pltpu.make_async_remote_copy(
            src_ref=ring.at[n_hops, span_of(chunk), :],
            dst_ref=swapped.at[span_of(chunk), :],
            send_sem=pool.at[n_hops * CHUNKS + chunk],
            recv_sem=swap_recv.at[chunk],
            device_id=partner,
            device_id_type=MESH,
        )

    def gather(chunk):
        span = slice(chunk * rows, (chunk + 1) * rows)
        swap_copy(chunk).wait_recv()
        total = ring[n_hops, span, :].astype(jnp.float32) + swapped[span, :].astype(jnp.float32)
        total = total + part[span, :]
        below_limit = live_rows - chunk * rows - lax.broadcasted_iota(jnp.int32, (rows, width), 0)
        before_limit = live_columns - lax.broadcasted_iota(jnp.int32, (rows, width), 1)
        live = jnp.minimum(jnp.maximum(jnp.minimum(below_limit, before_limit), 0), 1)
        grad[span, :] = (total * live.astype(jnp.float32)).astype(jnp.bfloat16)

    for chunk in range(CHUNKS):
        ring_copy(n_hops - 1, chunk).wait_recv()
        swap_copy(chunk).start()
        if chunk > 0:
            gather(chunk - 1)
    gather(CHUNKS - 1)

    deep = width // STRIPS
    strips = [slice(i * deep, (i + 1) * deep) for i in range(STRIPS)]

    def keep(strip, values):
        stat[strip, :] = values
        stat_bf[strip, :] = values.astype(jnp.bfloat16)

    @pl.when(core == 0)
    def _():
        for strip in strips:
            keep(strip, dot(grad[strip, :], grad[...], ROWS_BY_ROWS))

    @pl.when(core == 1)
    def _():
        for strip in strips:
            keep(strip, dot(grad[:, strip], grad[...], COLUMNS_BY_COLUMNS))

    def diagonal(strip):
        return (
            lax.broadcasted_iota(jnp.int32, (deep, width), 0) + strip.start
            == lax.broadcasted_iota(jnp.int32, (deep, width), 1)
        )

    for strip in strips:
        second[strip, :] = dot(stat_bf[strip, :], stat_bf[...])
    squares = jnp.zeros((1, 1), jnp.float32)
    trace = jnp.zeros((1, 1), jnp.float32)
    for strip in strips:
        values = stat[strip, :]
        squares += jnp.sum(values * values, keepdims=True)
        trace += jnp.sum(jnp.where(diagonal(strip), values, 0.0), keepdims=True)
    damping = DAMPING * (trace / width + 1e-06)
    norm_squared = squares + damping * (2.0 * trace + width * damping)
    inverse = lax.rsqrt(norm_squared)
    scale = lax.rsqrt(jnp.sqrt(jnp.sqrt(norm_squared)))

    for strip in strips:
        eye = jnp.where(diagonal(strip), damping, 0.0)
        values = stat[strip, :]
        square = (second[strip, :] + damping * (2.0 * values + eye)) * inverse * inverse
        values = (values + eye) * inverse
        stat[strip, :] = values
        stat_bf[strip, :] = values.astype(jnp.bfloat16)
        second[strip, :] = square
        second_bf[strip, :] = square.astype(jnp.bfloat16)
    for strip in strips:
        cube = dot(second_bf[strip, :], stat_bf[...])
        third_bf[strip, :] = cube.astype(jnp.bfloat16)
        one, two = stat[strip, :], second[strip, :]
        rest_bf[strip, :] = (ROOT[4] * one + ROOT[5] * two + ROOT[6] * cube).astype(jnp.bfloat16)
        lead = ROOT[1] * one + ROOT[2] * two + ROOT[3] * cube
        second[strip, :] = lead + jnp.where(diagonal(strip), ROOT[0], 0.0)

    def root(strip):
        values = second[strip, :] + dot(third_bf[strip, :], rest_bf[...])
        return (values * scale).astype(jnp.bfloat16)

    def right_copy(index):
        span = pl.ds(index * deep, deep)
        return pltpu.make_async_remote_copy(
            src_ref=right.at[span, :],
            dst_ref=right.at[span, :],
            send_sem=root_send.at[index],
            recv_sem=root_recv.at[index],
            device_id=partner,
            device_id_type=MESH,
        )

    weighted_copy = pltpu.make_async_remote_copy(
        src_ref=weighted_out,
        dst_ref=weighted,
        send_sem=root_send.at[STRIPS],
        recv_sem=root_recv.at[STRIPS],
        device_id=partner,
        device_id_type=MESH,
    )

    @pl.when(core == 1)
    def _():
        for index, strip in enumerate(strips):
            right[strip, :] = root(strip)
            right_copy(index).start()
        weighted_copy.wait_recv()

    @pl.when(core == 0)
    def _():
        for index, strip in enumerate(strips):
            place = index % (STRIPS // 2) * deep
            left[index // (STRIPS // 2), place : place + deep, :] = root(strip)
        weighted_out[...] = dot(left[1 - parity], grad[...]).astype(jnp.bfloat16)
        weighted_copy.start()
        weighted[...] = dot(left[parity], grad[...]).astype(jnp.bfloat16)
        for index in range(STRIPS):
            right_copy(index).wait_recv()

    @pl.loop(0, n_hops + 1)
    def _(item):
        pair_copy(item).wait_send()

    for chunk in range(few):
        ring_copy(0, core * few + chunk).wait_send()

    @pl.loop(1, n_hops)
    def _(step):
        for chunk in range(CHUNKS):
            ring_copy(step, chunk).wait_send()

    for chunk in range(CHUNKS):
        swap_copy(chunk).wait_send()

    piece = half // n_shard

    def update_rows(into):
        values = dot(weighted[...], right[...]) * math.sqrt(width)
        values = values.reshape(n_x, n_y, piece, width)
        for across in range(n_x):
            folded = jnp.concatenate([values[across, :, :, :half], values[across, :, :, half:]], axis=1)
            into[:, across] = folded.astype(jnp.bfloat16)

    far_first = sorted(range(n_y), key=lambda along: -min(along, n_y - along))
    far_first_x = sorted(range(n_x), key=lambda across: -min(across, n_x - across))

    def column(along):
        return lax.rem(y + along, n_y)

    def shift_copy(along):
        return pltpu.make_async_remote_copy(
            src_ref=rows_own.at[column(along)],
            dst_ref=rows_shift.at[column(along)],
            send_sem=shift_send.at[along],
            recv_sem=shift_recv.at[along],
            device_id=above,
            device_id_type=MESH,
        )

    def rows_copy(across, along):
        return pltpu.make_async_remote_copy(
            src_ref=rows_out.at[column(along), lax.rem(x + across, n_x)],
            dst_ref=out_ref.at[shard],
            send_sem=pool.at[across * n_y + along],
            recv_sem=rows_recv.at[along],
            device_id=(peer(across, along), rep),
            device_id_type=MESH,
        )

    own_copy = pltpu.make_async_copy(rows_out.at[y, x], out_ref.at[shard], pool.at[0])

    def send_rows(along):
        for across in far_first_x:
            if (across, along) == (0, 0):
                own_copy.start()
            else:
                rows_copy(across, along).start()

    @pl.when(core == 1)
    def _():
        update_rows(rows_out)
        for along in far_first:
            send_rows(along)

    @pl.when(core == 0)
    def _():
        update_rows(rows_own)
        for along in far_first:
            shift_copy(along).start()
        for along in far_first:
            shift_copy(along).wait_recv()
            place = column(along)
            moved = rows_shift[place].astype(jnp.float32)
            values = moved * odd + rows_own[place].astype(jnp.float32) * even
            rows_out[place] = values.astype(jnp.bfloat16)
            send_rows(along)

    own_copy.wait()

    for along in range(n_y):
        count = n_x - (along == 0)
        if count:
            pltpu.make_async_remote_copy(
                src_ref=rows_out.at[0, pl.ds(0, count)],
                dst_ref=out_ref.at[pl.ds(0, count)],
                send_sem=pool.at[0],
                recv_sem=rows_recv.at[along],
                device_id=partner,
                device_id_type=MESH,
            ).wait_recv()

    @pl.when(core == 1)
    def _():
        for index in range(STRIPS):
            right_copy(index).wait_send()

    @pl.when(core == 0)
    def _():
        weighted_copy.wait_send()
        for along in range(n_y):
            shift_copy(along).wait_send()

    for across in range(n_x):
        for along in range(n_y):
            if (across, along) != (0, 0):
                rows_copy(across, along).wait_send()


def local(n_shard, n_rep, acts, cotangents, block_shapes, owners):
    n_z = n_rep // 2
    n_x = 4 if n_shard == 32 else 1
    n_y = n_shard // n_x
    tokens, width = acts.shape[2:]
    half = width // 2
    n_hops = n_z // 2
    piece = half // n_shard
    bf16, f32 = jnp.bfloat16, jnp.float32
    dma = pltpu.SemaphoreType.DMA
    pieces = pltpu.VMEM((n_y, n_x, 2 * piece, half), bf16)
    rows = pl.pallas_call(
        functools.partial(kernel, n_z, n_x, n_y),
        out_shape=pltpu.VMEM((n_shard, 2 * piece, half), bf16),
        in_specs=[pl.BlockSpec(memory_space=pltpu.HBM)] * 4,
        out_specs=pl.BlockSpec(memory_space=pltpu.VMEM),
        scratch_shapes=[
            pltpu.SMEM(owners.shape, jnp.int32),
            pltpu.SMEM(block_shapes.shape[::-1], jnp.int32),
            pltpu.VMEM(acts.shape[1:], bf16),
            pltpu.VMEM(cotangents.shape[1:], bf16),
            pltpu.VMEM((n_hops + 1, tokens, 2 * width), bf16),
            pltpu.VMEM((n_hops + 1, 2 * tokens, 2 * width), bf16),
            pltpu.VMEM((width, width), f32),
            pltpu.VMEM((n_hops + 1, width, width), bf16),
            pltpu.VMEM((width, width), bf16),
            pltpu.VMEM((width, width), bf16),
            pltpu.VMEM((width, width), f32),
            pltpu.VMEM((width, width), bf16),
            pltpu.VMEM((width, width), f32),
            pltpu.VMEM((width, width), bf16),
            pltpu.VMEM((width, width), bf16),
            pltpu.VMEM((width, width), bf16),
            pltpu.VMEM((2, half, width), bf16),
            pltpu.VMEM((width, width), bf16),
            pltpu.VMEM((half, width), bf16),
            pltpu.VMEM((half, width), bf16),
            pieces,
            pieces,
            pieces,
            dma((max(n_shard, (n_hops + 1) * CHUNKS),)),
            dma((n_hops + 1,)),
            dma((n_hops, CHUNKS)),
            dma((CHUNKS,)),
            dma((STRIPS + 1,)),
            dma((STRIPS + 1,)),
            dma((max(n_y, n_hops + 1),)),
            dma((n_y,)),
            dma((n_y,)),
            pltpu.SemaphoreType.REGULAR((n_z // 2 - 1, 2)),
        ],
        compiler_params=pltpu.CompilerParams(
            collective_id=0, has_side_effects=True, vmem_limit_bytes=62 * 1024 * 1024
        ),
    )(owners, block_shapes.T, acts, cotangents)
    rows = rows.astype(f32).reshape(n_shard, 2, piece, half).transpose(0, 2, 1, 3)
    return rows.reshape(n_shard, 1, piece, width)


def solution(mesh):
    return jax.shard_map(
        functools.partial(local, mesh.shape["shard"], mesh.shape["rep"]),
        mesh=mesh,
        in_specs=(
            P("rep", "shard", None, None),
            P("rep", "shard", None, None),
            P("shard", None),
            P("shard"),
        ),
        out_specs=P(None, "rep", "shard", None),
        check_vma=False,
    )
```
